512 devices in a mesh: batch: 256 (over x, z_lo, y, core), mp: 2 (over z_hi).
Axes of the slice: x: 4, y: 4, z: 16 (z_hi: 2, z_lo: 8; z = z_hi * 8 + z_lo), core: 2. Of those that a mesh axis runs over, the one named last changes fastest.
Arguments:
- img_embed: bfloat16 [131072, 1152], P('batch', 'mp'), may hold values from -3 to 3
- txt_embed: bfloat16 [131072, 1152], P('batch', 'mp'), may hold values from -3 to 3
Outputs:
- img_grad: bfloat16 [131072, 1152], P('batch', 'mp')
- txt_grad: bfloat16 [131072, 1152], P('batch', 'mp')
The draws below stay inside these ranges and needn't reach their ends.
All inputs are finite; a program needn't handle non-finite values.
Results may differ from the reference program's by a relative error of at most 0.0079.
Values may be sent and summed in bfloat16 or wider, within the bound.
A program may use at most 64 MiB of HBM per device.

```python
import jax
import jax.numpy as jnp
from jax import lax

D = 1152
ROWS = 512
STEPS = 2
GLOBAL = 131072
N_BATCH = 256


def levels(rng, shape, pieces, low, largest):
    def one(dim, shards_of):
        heights = jax.random.uniform(jax.random.fold_in(jax.random.fold_in(rng, 6), dim), (shards_of,), jnp.float32, low / len(pieces), largest / len(pieces))
        return jnp.repeat(jnp.exp(heights), shape[dim] // shards_of).reshape((-1,) + (1,) * (len(shape) - dim - 1))

    level = one(*pieces[0])
    for cut in pieces[1:]:
        level = level * one(*cut)
    return level


def bell_draw(own_key, shape, scale, most, split=(), kind=jnp.bfloat16):
    level = levels(own_key, shape, split, -0.22, 0.18) if split else 1.0
    entries = jax.random.normal(own_key, shape, jnp.float32) * scale * level
    return jnp.minimum(jnp.maximum(entries, -most), most).astype(kind)


def setup_inputs(seed: int = 0) -> dict:
    splits = jax.random.split(jax.random.key(seed), 3)
    img_embed = bell_draw(splits[0], (GLOBAL, D), 0.5, 3.0, ((0, 256), (1, 2)))
    txt_embed = bell_draw(splits[1], (GLOBAL, D), 0.5, 3.0, ((0, 256), (1, 2)))
    return dict(img_embed=img_embed, txt_embed=txt_embed)


logit_scale = 100.0
logit_bias = -5.0
norm_eps = 1e-06

def contract_rows(left, right):
    return lax.dot_general(left, right, (((1,), (1,)), ((), ())), preferred_element_type=jnp.float32)

def pair_terms(image_block, caption_block, diagonal):
    scores = contract_rows(image_block, caption_block)
    weights = (jax.nn.sigmoid(logit_scale * scores + logit_bias) - diagonal).astype(jnp.bfloat16)
    image_part = logit_scale * jnp.dot(weights, caption_block, preferred_element_type=jnp.float32)
    caption_part = logit_scale * lax.dot_general(weights, image_block, (((0,), (0,)), ((), ())), preferred_element_type=jnp.float32)
    return (image_part, caption_part)

def unit_rows(embed):
    values = embed.astype(jnp.float32)
    inverse = lax.rsqrt(lax.optimization_barrier(jnp.sum(values * values, axis=1, keepdims=True)) + norm_eps)
    return (values * inverse, inverse)

def reference(img_embed, txt_embed):
    img_unit, img_inverse = unit_rows(img_embed)
    txt_unit, txt_inverse = unit_rows(txt_embed)
    width = img_embed.shape[1]
    img_blocks = img_unit.astype(jnp.bfloat16).reshape(N_BATCH, ROWS, width)
    txt_blocks = txt_unit.astype(jnp.bfloat16).reshape(N_BATCH, ROWS, width)
    img_total = jnp.zeros((N_BATCH, ROWS, width), jnp.float32)
    txt_total = jnp.zeros((N_BATCH, ROWS, width), jnp.float32)
    identity = jnp.eye(ROWS, dtype=jnp.float32)
    for offset in range(STEPS + 1):
        held_blocks = jnp.roll(txt_blocks, offset, axis=0)
        diagonal = identity if offset == 0 else jnp.zeros_like(identity)
        image_part, caption_part = lax.map(lambda operands: pair_terms(operands[0], operands[1], diagonal), (img_blocks, held_blocks))
        img_total = img_total + image_part
        txt_total = txt_total + jnp.roll(caption_part, -offset, axis=0)
    img_total = img_total.reshape(N_BATCH * ROWS, width)
    txt_total = txt_total.reshape(N_BATCH * ROWS, width)
    img_grad = (img_total - img_unit * lax.optimization_barrier(jnp.sum(img_unit * img_total, axis=1, keepdims=True))) * img_inverse
    txt_grad = (txt_total - txt_unit * lax.optimization_barrier(jnp.sum(txt_unit * txt_total, axis=1, keepdims=True))) * txt_inverse
    return (img_grad.astype(jnp.bfloat16), txt_grad.astype(jnp.bfloat16))
```

```python
import jax
import jax.numpy as jnp
from jax import lax
from jax.experimental import pallas as pl
from jax.experimental.pallas import tpu as pltpu
from jax.sharding import PartitionSpec as P

MESH = pl.DeviceIdType.MESH
BF16, F32 = jnp.bfloat16, jnp.float32

logit_scale = 100.0
logit_bias = -5.0
norm_eps = 1e-06

ROWS = 512
HALF = 576
MAIN = 512
REST = HALF - MAIN
FULL = 2 * HALF
CHUNK = 32
PACK = CHUNK // 2
STEPS = ROWS // 2 // CHUNK
ALL = 2 * STEPS
AHEAD = 3
LAND, RELAY, CHIP, CALC = 1, 2, 4, 5
LEG1, LEG2, HALO, VIA, PAIR = range(5)


def nt(left, right):
    return lax.dot_general(left, right, (((1,), (1,)), ((), ())), preferred_element_type=F32)


def weigh(scores):
    return 1.0 / (1.0 + jnp.exp(-(logit_scale * scores + logit_bias)))


def kernel(img_ref, txt_ref, img_out, txt_out, stage, land, full, inverse, txt_main, txt_rest, txt_inner, sent, came):
    batch, side = lax.axis_index("batch"), lax.axis_index("mp")
    core = lax.rem(batch, 2)
    y = lax.rem(lax.div(batch, 2), 4)
    z_lo = lax.rem(lax.div(batch, 8), 8)
    x = lax.div(batch, 64)
    z = side * 8 + z_lo

    def device(x, y, z, core):
        x, y, z = lax.rem(x + 4, 4), lax.rem(y + 4, 4), lax.rem(z + 16, 16)
        return (((x * 8 + lax.rem(z, 8)) * 4 + y) * 2 + core, lax.div(z, 8))

    def along_z(distance):
        return device(x, y, z + distance, core)

    x_next = x + lax.div(z_lo, 7)
    x_before = x - 1 + lax.div(z_lo + 7, 8)

    barrier = pltpu.get_barrier_semaphore()

    def greet(where):
        pl.semaphore_signal(barrier, inc=1, device_id=where, device_id_type=MESH)

    for distance in (1, -1, 7, -7):
        greet(along_z(distance))
    greet(device(x, y, z, 1 - core))
    for distance in (1, 2, 3):
        greet(device(x, y + distance, z, core))

    @pl.when(y == 0)
    def _():
        for column in range(4):
            greet(device(x_before, column, z - 1, core))

    @pl.when(y == 3)
    def _():
        for column in range(4):
            greet(device(x_next, column, z + 1, core))

    lane = lax.broadcasted_iota(jnp.int32, (PACK, 2 * REST), 1)

    def pack(ref, array):
        def one(chunk, carry):
            row = pl.multiple_of(chunk * CHUNK, CHUNK)
            low = ref[pl.ds(row, PACK), :]
            high = ref[pl.ds(row + PACK, PACK), :]
            stage[array, chunk, :, :MAIN] = low[:, :MAIN]
            stage[array, chunk, :, MAIN : 2 * MAIN] = high[:, :MAIN]
            stage[array, chunk, :, 2 * MAIN :] = jnp.concatenate([low[:, MAIN:], high[:, MAIN:]], axis=1)
            return carry

        lax.fori_loop(0, 2 * STEPS, one, 0)

    pack(txt_ref, 0)
    pack(img_ref, 1)
    txt_main[...] = jnp.zeros_like(txt_main)
    txt_rest[...] = jnp.zeros_like(txt_rest)
    txt_inner[...] = jnp.zeros_like(txt_inner)
    pl.semaphore_wait(barrier, 10)

    def split(t):
        return lax.div(t, STEPS), lax.rem(t, STEPS)

    def copy(kind, t, way, source, target, where):
        return pltpu.make_async_remote_copy(
            src_ref=source,
            dst_ref=target,
            send_sem=sent.at[kind, t, way],
            recv_sem=came.at[kind, t, way],
            device_id=where,
            device_id_type=MESH,
        )

    def first_leg(t, way):
        array, step = split(t)
        chunk = way * STEPS + step
        return copy(LEG1, t, way, stage.at[array, chunk], land.at[0, array, chunk], along_z(7 - 14 * way))

    def second_leg(t, way):
        array, step = split(t)
        chunk = way * STEPS + step
        return copy(LEG2, t, way, land.at[0, array, chunk], land.at[1, array, chunk], along_z(1 - 2 * way))

    def rows_of(t, way):
        array, step = split(t)
        return pl.ds(pl.multiple_of(way * (ROWS // 2) + step * CHUNK, CHUNK), CHUNK)

    def mirror(array, column):
        return column + array * (3 - 2 * column)

    def via_column(t, way):
        array, step = split(t)
        return lax.rem(2 * step + way, 4)

    def edge(array):
        return device(x_next + array * (x_before - x_next), 3 * array, z + 1 - 2 * array, core)

    def halo(t, way, where, source, target, kind):
        array, step = split(t)
        rows = rows_of(t, way)
        return copy(kind, t, way, full.at[source, rows], full.at[target, rows], where)

    def halo_start(t, way):
        array, step = split(t)
        own, next_one = 3 * array, 3 * array + 2
        place = mirror(array, y)
        via = via_column(t, way)

        @pl.when(place < 3)
        def _():
            halo(t, way, device(x, y + 1 - 2 * array, z, core), own, next_one, HALO).start()

        @pl.when(jnp.logical_and(place == 3, via == 3))
        def _():
            halo(t, way, edge(array), own, next_one, HALO).start()

        @pl.when(jnp.logical_and(place == 3, via < 3))
        def _():
            rows = rows_of(t, way)
            pltpu.make_async_remote_copy(
                src_ref=full.at[own, rows],
                dst_ref=full.at[6 + array, rows],
                send_sem=sent.at[HALO, t, way],
                recv_sem=came.at[VIA, t, way],
                device_id=device(x, mirror(array, via), z, core),
                device_id_type=MESH,
            ).start()

    def on_relay(t, way):
        array, step = split(t)
        via = via_column(t, way)
        return jnp.logical_and(mirror(array, y) == via, via < 3)

    def relay_copy(t, way):
        array, step = split(t)
        rows = rows_of(t, way)
        return pltpu.make_async_remote_copy(
            src_ref=full.at[6 + array, rows],
            dst_ref=full.at[3 * array + 2, rows],
            send_sem=sent.at[VIA, t, way],
            recv_sem=came.at[HALO, t, way],
            device_id=edge(array),
            device_id_type=MESH,
        )

    def pair_copy(t, way):
        array, step = split(t)
        source = 3 * array + 2 * (core + array * (1 - 2 * core))
        return halo(t, way, device(x, y, z, 1 - core), source, 3 * array + 1, PAIR)

    def arrive(t, way):
        array, step = split(t)
        chunk = way * STEPS + step
        row = pl.multiple_of(way * (ROWS // 2) + step * CHUNK, CHUNK)
        mine = stage[array, chunk].astype(F32)
        other = land[1, array, chunk].astype(F32)
        square = mine * mine + other * other
        rest_square = square[:, 2 * MAIN :]
        first = jnp.where(side == 0, mine[:, 2 * MAIN :], other[:, 2 * MAIN :])
        second = jnp.where(side == 0, other[:, 2 * MAIN :], mine[:, 2 * MAIN :])
        for part in range(2):
            total = jnp.sum(square[:, part * MAIN : (part + 1) * MAIN], axis=1, keepdims=True)
            inside = (lane < REST) if part == 0 else (lane >= REST)
            total = total + jnp.sum(jnp.where(inside, rest_square, 0.0), axis=1, keepdims=True)
            scale = lax.rsqrt(total + norm_eps)
            rows = pl.ds(pl.multiple_of(row + part * PACK, PACK), PACK)
            inverse[array, rows, :] = jnp.broadcast_to(scale, (PACK, 128))
            own = 3 * array
            mine_at = pl.ds(pl.multiple_of(side * MAIN, MAIN), MAIN)
            other_at = pl.ds(pl.multiple_of((1 - side) * MAIN, MAIN), MAIN)
            columns = slice(part * MAIN, (part + 1) * MAIN)
            full[own, rows, mine_at] = (mine[:, columns] * scale).astype(BF16)
            full[own, rows, other_at] = (other[:, columns] * scale).astype(BF16)
            if part == 0:
                rest = jnp.where(lane < REST, first, pltpu.roll(second, REST, 1))
            else:
                rest = jnp.where(lane < REST, pltpu.roll(first, REST, 1), second)
            full[own, rows, 2 * MAIN :] = (rest * scale).astype(BF16)

    main_at = pl.ds(pl.multiple_of(side * MAIN, MAIN), MAIN)

    def own_rest(rest):
        return jnp.where(side == 0, rest, pltpu.roll(rest, REST, 1))[:, :REST]

    def finish(ref, out, array, rows, main, rest, inner):
        scale = inverse[array, rows, :][:, :1]
        inner = logit_scale * inner
        values = ref[rows, :].astype(F32)
        unit = values[:, :MAIN] * scale
        out[rows, :MAIN] = ((logit_scale * main - unit * inner) * scale).astype(BF16)
        unit = values[:, MAIN:] * scale
        out[rows, MAIN:] = ((logit_scale * own_rest(rest) - unit * inner) * scale).astype(BF16)

    def images(t):
        both = [rows_of(t, way) for way in range(2)]
        array, step = split(t)
        block = jnp.concatenate([full[3, rows, :] for rows in both], axis=0)
        shape = (2 * CHUNK, ROWS)
        row = lax.broadcasted_iota(jnp.int32, shape, 0)
        row = row + step * CHUNK + jnp.where(row < CHUNK, 0, ROWS // 2 - CHUNK)
        matching = row == lax.broadcasted_iota(jnp.int32, shape, 1)
        main = jnp.zeros((2 * CHUNK, MAIN), F32)
        rest = jnp.zeros((2 * CHUNK, 2 * REST), F32)
        inner = jnp.zeros((2 * CHUNK, 1), F32)
        for offset in range(3):
            scores = nt(block, full[offset])
            weights = weigh(scores)
            if offset == 0:
                weights = jnp.where(matching, weights - 1.0, weights)
            inner = inner + jnp.sum(weights * scores, axis=1, keepdims=True)
            weights = weights.astype(BF16)
            main = main + jnp.dot(weights, full[offset, :, main_at], preferred_element_type=F32)
            rest = rest + jnp.dot(weights, full[offset, :, 2 * MAIN :], preferred_element_type=F32)
        for way, rows in enumerate(both):
            part = slice(way * CHUNK, (way + 1) * CHUNK)
            finish(img_ref, img_out, 1, rows, main[part], rest[part], inner[part])

    def captions(t):
        both = [rows_of(t, way) for way in range(2)]
        array, step = split(t)
        wide = 6 * CHUNK
        block = jnp.concatenate([full[3 + offset, rows, :] for offset in range(3) for rows in both], axis=0)
        block_main = jnp.concatenate([full[3 + offset, rows, main_at] for offset in range(3) for rows in both], axis=0)
        shape = (ROWS, wide)
        column = lax.broadcasted_iota(jnp.int32, shape, 1)
        place = column + step * CHUNK + jnp.where(column < CHUNK, 0, ROWS // 2 - CHUNK)
        matching = jnp.logical_and(column < 2 * CHUNK, place == lax.broadcasted_iota(jnp.int32, shape, 0))
        scores = nt(full[0], block)
        weights = weigh(scores)
        weights = jnp.where(matching, weights - 1.0, weights)
        txt_inner[...] += weights * scores
        weights = weights.astype(BF16)
        txt_main[...] += jnp.dot(weights, block_main, preferred_element_type=F32)
        txt_rest[...] += jnp.dot(weights, block[:, 2 * MAIN :], preferred_element_type=F32)

    for t in range(AHEAD):
        for way in range(2):
            first_leg(t, way).start()

    def during(t, body):
        @pl.when(jnp.logical_and(t >= 0, t < ALL))
        def _():
            for way in range(2):
                body(t, way)

    def step(now, carry):
        during(now + AHEAD, lambda t, way: first_leg(t, way).start())

        def pass_on(t, way):
            first_leg(t, way).wait_recv()
            second_leg(t, way).start()

        during(now, pass_on)

        def take(t, way):
            second_leg(t, way).wait_recv()
            arrive(t, way)
            halo_start(t, way)

        during(now - LAND, take)

        def relay(t, way):
            @pl.when(on_relay(t, way))
            def _():
                array, _ = split(t)
                rows = rows_of(t, way)
                halo(t, way, along_z(1), 6 + array, 6 + array, VIA).wait_recv()
                relay_copy(t, way).start()

        during(now - RELAY, relay)

        def to_pair(t, way):
            array, _ = split(t)
            halo(t, way, along_z(1), 3 * array, 3 * array + 2, HALO).wait_recv()
            pair_copy(t, way).start()

        during(now - CHIP, to_pair)

        t = now - CALC

        @pl.when(jnp.logical_and(t >= STEPS, t < ALL))
        def _():
            images(t)

        during(t, lambda t, way: pair_copy(t, way).wait_recv())

        @pl.when(jnp.logical_and(t >= STEPS, t < ALL))
        def _():
            captions(t)

        return carry

    lax.fori_loop(0, ALL + CALC, step, 0)

    def last(block, carry):
        rows = pl.ds(pl.multiple_of(block * 64, 64), 64)
        inner = jnp.sum(txt_inner[rows, :], axis=1, keepdims=True)
        finish(txt_ref, txt_out, 0, rows, txt_main[rows, :], txt_rest[rows, :], inner)
        return carry

    lax.fori_loop(0, ROWS // 64, last, 0)

    def drain(t, carry):
        array, _ = split(t)
        for way in range(2):
            first_leg(t, way).wait_send()
            second_leg(t, way).wait_send()
            halo(t, way, along_z(1), 3 * array, 3 * array + 2, HALO).wait_send()
            pair_copy(t, way).wait_send()

            @pl.when(on_relay(t, way))
            def _():
                relay_copy(t, way).wait_send()

        return carry

    lax.fori_loop(0, ALL, drain, 0)


def local(img_embed, txt_embed):
    vmem = pl.BlockSpec(memory_space=pltpu.VMEM)
    return pl.pallas_call(
        kernel,
        out_shape=(jax.ShapeDtypeStruct((ROWS, HALF), BF16),) * 2,
        in_specs=[vmem, vmem],
        out_specs=(vmem, vmem),
        scratch_shapes=[
            pltpu.VMEM((2, 2 * STEPS, PACK, FULL), BF16),
            pltpu.VMEM((2, 2, 2 * STEPS, PACK, FULL), BF16),
            pltpu.VMEM((8, ROWS, FULL), BF16),
            pltpu.VMEM((2, ROWS, 128), F32),
            pltpu.VMEM((ROWS, MAIN), F32),
            pltpu.VMEM((ROWS, 2 * REST), F32),
            pltpu.VMEM((ROWS, 6 * CHUNK), F32),
            pltpu.SemaphoreType.DMA((5, ALL, 2)),
            pltpu.SemaphoreType.DMA((5, ALL, 2)),
        ],
        compiler_params=pltpu.CompilerParams(
            collective_id=0, has_side_effects=True, vmem_limit_bytes=48 * 2**20
        ),
        name="gather_and_grad",
    )(img_embed, txt_embed)


def solution(mesh):
    return jax.shard_map(
        local,
        mesh=mesh,
        in_specs=(P("batch", "mp"), P("batch", "mp")),
        out_specs=(P("batch", "mp"), P("batch", "mp")),
        check_vma=False,
    )
```

```python
import jax
import jax.numpy as jnp
from jax import lax
from jax.experimental import pallas as pl
from jax.experimental.pallas import tpu as pltpu
from jax.sharding import PartitionSpec as P

MESH = pl.DeviceIdType.MESH
BF16, F32 = jnp.bfloat16, jnp.float32

logit_scale = 100.0
logit_bias = -5.0
norm_eps = 1e-06

ROWS = 512
HALF = 576
MAIN = 512
REST = HALF - MAIN
FULL = 2 * HALF
CHUNK = 32
PACK = CHUNK // 2
STEPS = ROWS // 2 // CHUNK
ALL = 2 * STEPS
AHEAD = 3
LAND, RELAY, CHIP, CALC = 1, 2, 3, 4
LEG1, LEG2, HALO, VIA, PAIR = range(5)


def nt(left, right):
    return lax.dot_general(left, right, (((1,), (1,)), ((), ())), preferred_element_type=F32)


def weigh(scores):
    return 1.0 / (1.0 + jnp.exp(-(logit_scale * scores + logit_bias)))


def kernel(
    img_hbm, txt_hbm, img_out, txt_out, img_ref, txt_ref, stage, land, full, inverse, txt_main, txt_rest, txt_inner,
    sent, came, load,
):
    batch, side = lax.axis_index("batch"), lax.axis_index("mp")
    core = lax.rem(batch, 2)
    y = lax.rem(lax.div(batch, 2), 4)
    z_lo = lax.rem(lax.div(batch, 8), 8)
    x = lax.div(batch, 64)
    z = side * 8 + z_lo

    def device(x, y, z, core):
        x, y, z = lax.rem(x + 4, 4), lax.rem(y + 4, 4), lax.rem(z + 16, 16)
        return (((x * 8 + lax.rem(z, 8)) * 4 + y) * 2 + core, lax.div(z, 8))

    def along_z(distance):
        return device(x, y, z + distance, core)

    x_next = x + lax.div(z_lo, 7)
    x_before = x - 1 + lax.div(z_lo + 7, 8)

    barrier = pltpu.get_barrier_semaphore()

    def greet(where):
        pl.semaphore_signal(barrier, inc=1, device_id=where, device_id_type=MESH)

    for distance in (1, -1, 7, -7):
        greet(along_z(distance))
    greet(device(x, y, z, 1 - core))
    for distance in (1, 2, 3):
        greet(device(x, y + distance, z, core))

    @pl.when(y == 0)
    def _():
        for column in range(4):
            greet(device(x_before, column, z - 1, core))

    @pl.when(y == 3)
    def _():
        for column in range(4):
            greet(device(x_next, column, z + 1, core))

    lane = lax.broadcasted_iota(jnp.int32, (PACK, 2 * REST), 1)

    txt_load = pltpu.make_async_copy(txt_hbm, txt_ref, load.at[0])
    img_load = pltpu.make_async_copy(img_hbm, img_ref, load.at[1])
    txt_load.start()
    img_load.start()

    def pack(ref, array):
        def one(chunk, carry):
            row = pl.multiple_of(chunk * CHUNK, CHUNK)
            low = ref[pl.ds(row, PACK), :]
            high = ref[pl.ds(row + PACK, PACK), :]
            stage[array, chunk, :, :MAIN] = low[:, :MAIN]
            stage[array, chunk, :, MAIN : 2 * MAIN] = high[:, :MAIN]
            stage[array, chunk, :, 2 * MAIN :] = jnp.concatenate([low[:, MAIN:], high[:, MAIN:]], axis=1)
            return carry

        lax.fori_loop(0, 2 * STEPS, one, 0)

    txt_load.wait()
    pack(txt_ref, 0)
    pl.semaphore_wait(barrier, 10)

    def split(t):
        return lax.div(t, STEPS), lax.rem(t, STEPS)

    def copy(kind, t, way, source, target, where):
        return pltpu.make_async_remote_copy(
            src_ref=source,
            dst_ref=target,
            send_sem=sent.at[kind, t, way],
            recv_sem=came.at[kind, t, way],
            device_id=where,
            device_id_type=MESH,
        )

    def first_leg(t, way):
        array, step = split(t)
        chunk = way * STEPS + step
        return copy(LEG1, t, way, stage.at[array, chunk], land.at[0, array, chunk], along_z(7 - 14 * way))

    def second_leg(t, way):
        array, step = split(t)
        chunk = way * STEPS + step
        return copy(LEG2, t, way, land.at[0, array, chunk], land.at[1, array, chunk], along_z(1 - 2 * way))

    def rows_of(t, way):
        array, step = split(t)
        return pl.ds(pl.multiple_of(way * (ROWS // 2) + step * CHUNK, CHUNK), CHUNK)

    def mirror(array, column):
        return column + array * (3 - 2 * column)

    def via_column(t, way):
        array, step = split(t)
        via = lax.rem(2 * step + way, 4)
        return via + array * lax.div(step, STEPS - 1) * (3 - via)

    def edge(array):
        return device(x_next + array * (x_before - x_next), 3 * array, z + 1 - 2 * array, core)

    def halo(t, way, where, source, target, kind):
        array, step = split(t)
        rows = rows_of(t, way)
        return copy(kind, t, way, full.at[source, rows], full.at[target, rows], where)

    def halo_start(t, way):
        array, step = split(t)
        own, next_one = 3 * array, 3 * array + 2
        place = mirror(array, y)
        via = via_column(t, way)

        @pl.when(place < 3)
        def _():
            halo(t, way, device(x, y + 1 - 2 * array, z, core), own, next_one, HALO).start()

        @pl.when(jnp.logical_and(place == 3, via == 3))
        def _():
            halo(t, way, edge(array), own, next_one, HALO).start()

        @pl.when(jnp.logical_and(place == 3, via < 3))
        def _():
            rows = rows_of(t, way)
            pltpu.make_async_remote_copy(
                src_ref=full.at[own, rows],
                dst_ref=full.at[6 + array, rows],
                send_sem=sent.at[HALO, t, way],
                recv_sem=came.at[VIA, t, way],
                device_id=device(x, mirror(array, via), z, core),
                device_id_type=MESH,
            ).start()

    def on_relay(t, way):
        array, step = split(t)
        via = via_column(t, way)
        return jnp.logical_and(mirror(array, y) == via, via < 3)

    def relay_copy(t, way):
        array, step = split(t)
        rows = rows_of(t, way)
        return pltpu.make_async_remote_copy(
            src_ref=full.at[6 + array, rows],
            dst_ref=full.at[3 * array + 2, rows],
            send_sem=sent.at[VIA, t, way],
            recv_sem=came.at[HALO, t, way],
            device_id=edge(array),
            device_id_type=MESH,
        )

    def pair_copy(t, way):
        array, step = split(t)
        source = 3 * array + 2 * (core + array * (1 - 2 * core))
        return halo(t, way, device(x, y, z, 1 - core), source, 3 * array + 1, PAIR)

    def arrive(t, way):
        array, step = split(t)
        chunk = way * STEPS + step
        row = pl.multiple_of(way * (ROWS // 2) + step * CHUNK, CHUNK)
        mine = stage[array, chunk].astype(F32)
        other = land[1, array, chunk].astype(F32)
        square = mine * mine + other * other
        rest_square = square[:, 2 * MAIN :]
        first = jnp.where(side == 0, mine[:, 2 * MAIN :], other[:, 2 * MAIN :])
        second = jnp.where(side == 0, other[:, 2 * MAIN :], mine[:, 2 * MAIN :])
        for part in range(2):
            total = jnp.sum(square[:, part * MAIN : (part + 1) * MAIN], axis=1, keepdims=True)
            inside = (lane < REST) if part == 0 else (lane >= REST)
            total = total + jnp.sum(jnp.where(inside, rest_square, 0.0), axis=1, keepdims=True)
            scale = lax.rsqrt(total + norm_eps)
            rows = pl.ds(pl.multiple_of(row + part * PACK, PACK), PACK)
            inverse[array, rows, :] = jnp.broadcast_to(scale, (PACK, 128))
            own = 3 * array
            mine_at = pl.ds(pl.multiple_of(side * MAIN, MAIN), MAIN)
            other_at = pl.ds(pl.multiple_of((1 - side) * MAIN, MAIN), MAIN)
            columns = slice(part * MAIN, (part + 1) * MAIN)
            full[own, rows, mine_at] = (mine[:, columns] * scale).astype(BF16)
            full[own, rows, other_at] = (other[:, columns] * scale).astype(BF16)
            if part == 0:
                rest = jnp.where(lane < REST, first, pltpu.roll(second, REST, 1))
            else:
                rest = jnp.where(lane < REST, pltpu.roll(first, REST, 1), second)
            full[own, rows, 2 * MAIN :] = (rest * scale).astype(BF16)

    main_at = pl.ds(pl.multiple_of(side * MAIN, MAIN), MAIN)

    def own_rest(rest):
        return jnp.where(side == 0, rest, pltpu.roll(rest, REST, 1))[:, :REST]

    def finish(ref, out, array, rows, main, rest, inner):
        scale = inverse[array, rows, :][:, :1]
        inner = logit_scale * inner
        values = ref[rows, :].astype(F32)
        unit = values[:, :MAIN] * scale
        out[rows, :MAIN] = ((logit_scale * main - unit * inner) * scale).astype(BF16)
        unit = values[:, MAIN:] * scale
        out[rows, MAIN:] = ((logit_scale * own_rest(rest) - unit * inner) * scale).astype(BF16)

    def images(t):
        both = [rows_of(t, way) for way in range(2)]
        array, step = split(t)
        block = jnp.concatenate([full[3, rows, :] for rows in both], axis=0)
        shape = (2 * CHUNK, ROWS)
        row = lax.broadcasted_iota(jnp.int32, shape, 0)
        row = row + step * CHUNK + jnp.where(row < CHUNK, 0, ROWS // 2 - CHUNK)
        matching = row == lax.broadcasted_iota(jnp.int32, shape, 1)
        main = jnp.zeros((2 * CHUNK, MAIN), F32)
        rest = jnp.zeros((2 * CHUNK, 2 * REST), F32)
        inner = jnp.zeros((2 * CHUNK, 1), F32)
        for offset in range(3):
            scores = nt(block, full[offset])
            weights = weigh(scores)
            if offset == 0:
                weights = jnp.where(matching, weights - 1.0, weights)
            inner = inner + jnp.sum(weights * scores, axis=1, keepdims=True)
            weights = weights.astype(BF16)
            main = main + jnp.dot(weights, full[offset, :, main_at], preferred_element_type=F32)
            rest = rest + jnp.dot(weights, full[offset, :, 2 * MAIN :], preferred_element_type=F32)
        for way, rows in enumerate(both):
            part = slice(way * CHUNK, (way + 1) * CHUNK)
            finish(img_ref, img_out, 1, rows, main[part], rest[part], inner[part])

    def captions(t):
        both = [rows_of(t, way) for way in range(2)]
        array, step = split(t)
        wide = 6 * CHUNK
        block = jnp.concatenate([full[3 + offset, rows, :] for offset in range(3) for rows in both], axis=0)
        block_main = jnp.concatenate([full[3 + offset, rows, main_at] for offset in range(3) for rows in both], axis=0)
        shape = (ROWS, wide)
        column = lax.broadcasted_iota(jnp.int32, shape, 1)
        place = column + step * CHUNK + jnp.where(column < CHUNK, 0, ROWS // 2 - CHUNK)
        matching = jnp.logical_and(column < 2 * CHUNK, place == lax.broadcasted_iota(jnp.int32, shape, 0))
        scores = nt(full[0], block)
        weights = weigh(scores)
        weights = jnp.where(matching, weights - 1.0, weights)
        txt_inner[...] += weights * scores
        weights = weights.astype(BF16)
        txt_main[...] += jnp.dot(weights, block_main, preferred_element_type=F32)
        txt_rest[...] += jnp.dot(weights, block[:, 2 * MAIN :], preferred_element_type=F32)

    for t in range(AHEAD):
        for way in range(2):
            first_leg(t, way).start()

    img_load.wait()
    pack(img_ref, 1)
    txt_main[...] = jnp.zeros_like(txt_main)
    txt_rest[...] = jnp.zeros_like(txt_rest)
    txt_inner[...] = jnp.zeros_like(txt_inner)

    def during(t, body):
        @pl.when(jnp.logical_and(t >= 0, t < ALL))
        def _():
            for way in range(2):
                body(t, way)

    def step(now, carry):
        def pass_on(t, way):
            first_leg(t, way).wait_recv()
            second_leg(t, way).start()

        during(now, pass_on)
        during(now + AHEAD, lambda t, way: first_leg(t, way).start())

        def take(t, way):
            second_leg(t, way).wait_recv()
            arrive(t, way)
            halo_start(t, way)

        during(now - LAND, take)

        def relay(t, way):
            @pl.when(on_relay(t, way))
            def _():
                array, _ = split(t)
                rows = rows_of(t, way)
                halo(t, way, along_z(1), 6 + array, 6 + array, VIA).wait_recv()
                relay_copy(t, way).start()

        during(now - RELAY, relay)

        def to_pair(t, way):
            array, _ = split(t)
            halo(t, way, along_z(1), 3 * array, 3 * array + 2, HALO).wait_recv()
            pair_copy(t, way).start()

        during(now - CHIP, to_pair)

        during(now - CALC, lambda t, way: pair_copy(t, way).wait_recv())
        before = now - CALC

        @pl.when(jnp.logical_and(before >= STEPS, before < ALL))
        def _():
            captions(before)

        before_pair = now - CHIP

        @pl.when(jnp.logical_and(before_pair >= STEPS, before_pair < ALL))
        def _():
            images(before_pair)

        return carry

    lax.fori_loop(0, ALL + CALC, step, 0)

    def last(block, carry):
        rows = pl.ds(pl.multiple_of(block * 64, 64), 64)
        inner = jnp.sum(txt_inner[rows, :], axis=1, keepdims=True)
        finish(txt_ref, txt_out, 0, rows, txt_main[rows, :], txt_rest[rows, :], inner)
        return carry

    lax.fori_loop(0, ROWS // 64, last, 0)

    def drain(t, carry):
        array, _ = split(t)
        for way in range(2):
            first_leg(t, way).wait_send()
            second_leg(t, way).wait_send()
            halo(t, way, along_z(1), 3 * array, 3 * array + 2, HALO).wait_send()
            pair_copy(t, way).wait_send()

            @pl.when(on_relay(t, way))
            def _():
                relay_copy(t, way).wait_send()

        return carry

    lax.fori_loop(0, ALL, drain, 0)


def local(img_embed, txt_embed):
    vmem = pl.BlockSpec(memory_space=pltpu.VMEM)
    return pl.pallas_call(
        kernel,
        out_shape=(jax.ShapeDtypeStruct((ROWS, HALF), BF16),) * 2,
        in_specs=[pl.BlockSpec(memory_space=pl.ANY)] * 2,
        out_specs=(vmem, vmem),
        scratch_shapes=[
            pltpu.VMEM((ROWS, HALF), BF16),
            pltpu.VMEM((ROWS, HALF), BF16),
            pltpu.VMEM((2, 2 * STEPS, PACK, FULL), BF16),
            pltpu.VMEM((2, 2, 2 * STEPS, PACK, FULL), BF16),
            pltpu.VMEM((8, ROWS, FULL), BF16),
            pltpu.VMEM((2, ROWS, 128), F32),
            pltpu.VMEM((ROWS, MAIN), F32),
            pltpu.VMEM((ROWS, 2 * REST), F32),
            pltpu.VMEM((ROWS, 6 * CHUNK), F32),
            pltpu.SemaphoreType.DMA((5, ALL, 2)),
            pltpu.SemaphoreType.DMA((5, ALL, 2)),
            pltpu.SemaphoreType.DMA((2,)),
        ],
        compiler_params=pltpu.CompilerParams(
            collective_id=0, has_side_effects=True, vmem_limit_bytes=48 * 2**20
        ),
        name="gather_and_grad",
    )(img_embed, txt_embed)


def solution(mesh):
    return jax.shard_map(
        local,
        mesh=mesh,
        in_specs=(P("batch", "mp"), P("batch", "mp")),
        out_specs=(P("batch", "mp"), P("batch", "mp")),
        check_vma=False,
    )
```

```python
import jax
import jax.numpy as jnp
from jax import lax
from jax.experimental import pallas as pl
from jax.experimental.pallas import tpu as pltpu
from jax.sharding import PartitionSpec as P

MESH = pl.DeviceIdType.MESH
BF16, F32 = jnp.bfloat16, jnp.float32

logit_scale = 100.0
logit_bias = -5.0
norm_eps = 1e-06

ROWS = 512
HALF = 576
MAIN = 512
REST = HALF - MAIN
FULL = 2 * HALF
CHUNK = 32
PACK = CHUNK // 2
STEPS = ROWS // 2 // CHUNK
ALL = 2 * STEPS
AHEAD = 3
LAND, RELAY, CHIP, CALC = 1, 2, 3, 4
LEG1, LEG2, HALO, VIA, PAIR = range(5)


def nt(left, right):
    return lax.dot_general(left, right, (((1,), (1,)), ((), ())), preferred_element_type=F32)


def weigh(scores):
    return 1.0 / (1.0 + jnp.exp(-(logit_scale * scores + logit_bias)))


def kernel(
    img_hbm, txt_hbm, img_out, txt_out, img_ref, txt_ref, stage, land, full, inverse, txt_main, txt_rest, txt_inner,
    sent, came, load,
):
    batch, side = lax.axis_index("batch"), lax.axis_index("mp")
    core = lax.rem(batch, 2)
    y = lax.rem(lax.div(batch, 2), 4)
    z_lo = lax.rem(lax.div(batch, 8), 8)
    x = lax.div(batch, 64)
    z = side * 8 + z_lo

    def device(x, y, z, core):
        x, y, z = lax.rem(x + 4, 4), lax.rem(y + 4, 4), lax.rem(z + 16, 16)
        return (((x * 8 + lax.rem(z, 8)) * 4 + y) * 2 + core, lax.div(z, 8))

    def along_z(distance):
        return device(x, y, z + distance, core)

    x_next = x + lax.div(z_lo, 7)
    x_before = x - 1 + lax.div(z_lo + 7, 8)

    barrier = pltpu.get_barrier_semaphore()

    def greet(where):
        pl.semaphore_signal(barrier, inc=1, device_id=where, device_id_type=MESH)

    for distance in (1, -1, 7, -7):
        greet(along_z(distance))
    greet(device(x, y, z, 1 - core))
    for distance in (1, 2, 3):
        greet(device(x, y + distance, z, core))

    @pl.when(y == 0)
    def _():
        for column in range(4):
            greet(device(x_before, column, z - 1, core))

    @pl.when(y == 3)
    def _():
        for column in range(4):
            greet(device(x_next, column, z + 1, core))

    lane = lax.broadcasted_iota(jnp.int32, (PACK, 2 * REST), 1)

    txt_load = pltpu.make_async_copy(txt_hbm, txt_ref, load.at[0])
    img_load = pltpu.make_async_copy(img_hbm, img_ref, load.at[1])
    txt_load.start()
    img_load.start()

    def pack(ref, array):
        def one(chunk, carry):
            row = pl.multiple_of(chunk * CHUNK, CHUNK)
            low = ref[pl.ds(row, PACK), :]
            high = ref[pl.ds(row + PACK, PACK), :]
            stage[array, chunk, :, :MAIN] = low[:, :MAIN]
            stage[array, chunk, :, MAIN : 2 * MAIN] = high[:, :MAIN]
            stage[array, chunk, :, 2 * MAIN :] = jnp.concatenate([low[:, MAIN:], high[:, MAIN:]], axis=1)
            return carry

        lax.fori_loop(0, 2 * STEPS, one, 0)

    txt_load.wait()
    pack(txt_ref, 0)
    pl.semaphore_wait(barrier, 10)

    def split(t):
        return lax.div(t, STEPS), lax.rem(t, STEPS)

    def copy(kind, t, way, source, target, where):
        return pltpu.make_async_remote_copy(
            src_ref=source,
            dst_ref=target,
            send_sem=sent.at[kind, t, way],
            recv_sem=came.at[kind, t, way],
            device_id=where,
            device_id_type=MESH,
        )

    def first_leg(t, way):
        array, step = split(t)
        chunk = way * STEPS + step
        return copy(LEG1, t, way, stage.at[array, chunk], land.at[0, array, chunk], along_z(7 - 14 * way))

    def second_leg(t, way):
        array, step = split(t)
        chunk = way * STEPS + step
        return copy(LEG2, t, way, land.at[0, array, chunk], land.at[1, array, chunk], along_z(1 - 2 * way))

    def rows_of(t, way):
        array, step = split(t)
        return pl.ds(pl.multiple_of(way * (ROWS // 2) + step * CHUNK, CHUNK), CHUNK)

    def mirror(array, column):
        return column + array * (3 - 2 * column)

    def via_column(t, way):
        array, step = split(t)
        spread = lax.rem(2 * step + way, 4)
        late = lax.div(step, STEPS - 2)
        others = lax.rem(2 * step + way, 3)
        return spread + array * (others + late * (3 - others) - spread)

    def edge(array):
        return device(x_next + array * (x_before - x_next), 3 * array, z + 1 - 2 * array, core)

    def halo(t, way, where, source, target, kind):
        array, step = split(t)
        rows = rows_of(t, way)
        return copy(kind, t, way, full.at[source, rows], full.at[target, rows], where)

    def halo_start(t, way):
        array, step = split(t)
        own, next_one = 3 * array, 3 * array + 2
        place = mirror(array, y)
        via = via_column(t, way)

        @pl.when(place < 3)
        def _():
            halo(t, way, device(x, y + 1 - 2 * array, z, core), own, next_one, HALO).start()

        @pl.when(jnp.logical_and(place == 3, via == 3))
        def _():
            halo(t, way, edge(array), own, next_one, HALO).start()

        @pl.when(jnp.logical_and(place == 3, via < 3))
        def _():
            rows = rows_of(t, way)
            pltpu.make_async_remote_copy(
                src_ref=full.at[own, rows],
                dst_ref=full.at[6 + array, rows],
                send_sem=sent.at[HALO, t, way],
                recv_sem=came.at[VIA, t, way],
                device_id=device(x, mirror(array, via), z, core),
                device_id_type=MESH,
            ).start()

    def on_relay(t, way):
        array, step = split(t)
        via = via_column(t, way)
        return jnp.logical_and(mirror(array, y) == via, via < 3)

    def relay_copy(t, way):
        array, step = split(t)
        rows = rows_of(t, way)
        return pltpu.make_async_remote_copy(
            src_ref=full.at[6 + array, rows],
            dst_ref=full.at[3 * array + 2, rows],
            send_sem=sent.at[VIA, t, way],
            recv_sem=came.at[HALO, t, way],
            device_id=edge(array),
            device_id_type=MESH,
        )

    def pair_copy(t, way):
        array, step = split(t)
        source = 3 * array + 2 * (core + array * (1 - 2 * core))
        return halo(t, way, device(x, y, z, 1 - core), source, 3 * array + 1, PAIR)

    def arrive(t, way):
        array, step = split(t)
        chunk = way * STEPS + step
        row = pl.multiple_of(way * (ROWS // 2) + step * CHUNK, CHUNK)
        mine = stage[array, chunk].astype(F32)
        other = land[1, array, chunk].astype(F32)
        square = mine * mine + other * other
        rest_square = square[:, 2 * MAIN :]
        first = jnp.where(side == 0, mine[:, 2 * MAIN :], other[:, 2 * MAIN :])
        second = jnp.where(side == 0, other[:, 2 * MAIN :], mine[:, 2 * MAIN :])
        for part in range(2):
            total = jnp.sum(square[:, part * MAIN : (part + 1) * MAIN], axis=1, keepdims=True)
            inside = (lane < REST) if part == 0 else (lane >= REST)
            total = total + jnp.sum(jnp.where(inside, rest_square, 0.0), axis=1, keepdims=True)
            scale = lax.rsqrt(total + norm_eps)
            rows = pl.ds(pl.multiple_of(row + part * PACK, PACK), PACK)
            inverse[array, rows, :] = jnp.broadcast_to(scale, (PACK, 128))
            own = 3 * array
            mine_at = pl.ds(pl.multiple_of(side * MAIN, MAIN), MAIN)
            other_at = pl.ds(pl.multiple_of((1 - side) * MAIN, MAIN), MAIN)
            columns = slice(part * MAIN, (part + 1) * MAIN)
            full[own, rows, mine_at] = (mine[:, columns] * scale).astype(BF16)
            full[own, rows, other_at] = (other[:, columns] * scale).astype(BF16)
            if part == 0:
                rest = jnp.where(lane < REST, first, pltpu.roll(second, REST, 1))
            else:
                rest = jnp.where(lane < REST, pltpu.roll(first, REST, 1), second)
            full[own, rows, 2 * MAIN :] = (rest * scale).astype(BF16)

    main_at = pl.ds(pl.multiple_of(side * MAIN, MAIN), MAIN)

    def own_rest(rest):
        return jnp.where(side == 0, rest, pltpu.roll(rest, REST, 1))[:, :REST]

    def finish(ref, out, array, rows, main, rest, inner):
        scale = inverse[array, rows, :][:, :1]
        inner = logit_scale * inner
        values = ref[rows, :].astype(F32)
        unit = values[:, :MAIN] * scale
        out[rows, :MAIN] = ((logit_scale * main - unit * inner) * scale).astype(BF16)
        unit = values[:, MAIN:] * scale
        out[rows, MAIN:] = ((logit_scale * own_rest(rest) - unit * inner) * scale).astype(BF16)

    def images(t):
        both = [rows_of(t, way) for way in range(2)]
        array, step = split(t)
        block = jnp.concatenate([full[3, rows, :] for rows in both], axis=0)
        shape = (2 * CHUNK, ROWS)
        row = lax.broadcasted_iota(jnp.int32, shape, 0)
        row = row + step * CHUNK + jnp.where(row < CHUNK, 0, ROWS // 2 - CHUNK)
        matching = row == lax.broadcasted_iota(jnp.int32, shape, 1)
        main = jnp.zeros((2 * CHUNK, MAIN), F32)
        rest = jnp.zeros((2 * CHUNK, 2 * REST), F32)
        inner = jnp.zeros((2 * CHUNK, 1), F32)
        for offset in range(3):
            scores = nt(block, full[offset])
            weights = weigh(scores)
            if offset == 0:
                weights = jnp.where(matching, weights - 1.0, weights)
            inner = inner + jnp.sum(weights * scores, axis=1, keepdims=True)
            weights = weights.astype(BF16)
            main = main + jnp.dot(weights, full[offset, :, main_at], preferred_element_type=F32)
            rest = rest + jnp.dot(weights, full[offset, :, 2 * MAIN :], preferred_element_type=F32)
        for way, rows in enumerate(both):
            part = slice(way * CHUNK, (way + 1) * CHUNK)
            finish(img_ref, img_out, 1, rows, main[part], rest[part], inner[part])

    def captions(t):
        both = [rows_of(t, way) for way in range(2)]
        array, step = split(t)
        wide = 6 * CHUNK
        block = jnp.concatenate([full[3 + offset, rows, :] for offset in range(3) for rows in both], axis=0)
        block_main = jnp.concatenate([full[3 + offset, rows, main_at] for offset in range(3) for rows in both], axis=0)
        shape = (ROWS, wide)
        column = lax.broadcasted_iota(jnp.int32, shape, 1)
        place = column + step * CHUNK + jnp.where(column < CHUNK, 0, ROWS // 2 - CHUNK)
        matching = jnp.logical_and(column < 2 * CHUNK, place == lax.broadcasted_iota(jnp.int32, shape, 0))
        scores = nt(full[0], block)
        weights = weigh(scores)
        weights = jnp.where(matching, weights - 1.0, weights)
        txt_inner[...] += weights * scores
        weights = weights.astype(BF16)
        txt_main[...] += jnp.dot(weights, block_main, preferred_element_type=F32)
        txt_rest[...] += jnp.dot(weights, block[:, 2 * MAIN :], preferred_element_type=F32)

    for t in range(AHEAD):
        for way in range(2):
            first_leg(t, way).start()

    img_load.wait()
    pack(img_ref, 1)
    txt_main[...] = jnp.zeros_like(txt_main)
    txt_rest[...] = jnp.zeros_like(txt_rest)
    txt_inner[...] = jnp.zeros_like(txt_inner)

    def during(t, body):
        @pl.when(jnp.logical_and(t >= 0, t < ALL))
        def _():
            for way in range(2):
                body(t, way)

    def done_before(now):
        level = lax.div(now, ALL - 1)
        return (2 * now - ALL + 1) * (1 - level) + (now - 1) * level

    def step(now, carry):
        def pass_on(t, way):
            first_leg(t, way).wait_recv()
            second_leg(t, way).start()

        during(now, pass_on)
        during(now + AHEAD, lambda t, way: first_leg(t, way).start())

        def take(t, way):
            second_leg(t, way).wait_recv()
            arrive(t, way)
            halo_start(t, way)

        during(now - LAND, take)

        def relay(t, way):
            @pl.when(on_relay(t, way))
            def _():
                array, _ = split(t)
                rows = rows_of(t, way)
                halo(t, way, along_z(1), 6 + array, 6 + array, VIA).wait_recv()
                relay_copy(t, way).start()

        during(now - RELAY, relay)

        def to_pair(t, way):
            array, _ = split(t)
            halo(t, way, along_z(1), 3 * array, 3 * array + 2, HALO).wait_recv()
            pair_copy(t, way).start()

        during(now - CHIP, to_pair)
        during(now - CALC, lambda t, way: pair_copy(t, way).wait_recv())
        before = now - CALC

        @pl.when(jnp.logical_and(before >= STEPS, before < ALL))
        def _():
            captions(before)

        @pl.when(jnp.logical_and(now >= STEPS + CHIP, now <= ALL))
        def _():
            def rows(t, carry):
                @pl.when(t >= STEPS)
                def _():
                    images(t)

                return carry

            lax.fori_loop(done_before(now), done_before(now + 1), rows, 0)

        return carry

    lax.fori_loop(0, ALL + CALC, step, 0)

    def last(block, carry):
        rows = pl.ds(pl.multiple_of(block * 64, 64), 64)
        inner = jnp.sum(txt_inner[rows, :], axis=1, keepdims=True)
        finish(txt_ref, txt_out, 0, rows, txt_main[rows, :], txt_rest[rows, :], inner)
        return carry

    lax.fori_loop(0, ROWS // 64, last, 0)

    def drain(t, carry):
        array, _ = split(t)
        for way in range(2):
            first_leg(t, way).wait_send()
            second_leg(t, way).wait_send()
            halo(t, way, along_z(1), 3 * array, 3 * array + 2, HALO).wait_send()
            pair_copy(t, way).wait_send()

            @pl.when(on_relay(t, way))
            def _():
                relay_copy(t, way).wait_send()

        return carry

    lax.fori_loop(0, ALL, drain, 0)


def local(img_embed, txt_embed):
    vmem = pl.BlockSpec(memory_space=pltpu.VMEM)
    return pl.pallas_call(
        kernel,
        out_shape=(jax.ShapeDtypeStruct((ROWS, HALF), BF16),) * 2,
        in_specs=[pl.BlockSpec(memory_space=pl.ANY)] * 2,
        out_specs=(vmem, vmem),
        scratch_shapes=[
            pltpu.VMEM((ROWS, HALF), BF16),
            pltpu.VMEM((ROWS, HALF), BF16),
            pltpu.VMEM((2, 2 * STEPS, PACK, FULL), BF16),
            pltpu.VMEM((2, 2, 2 * STEPS, PACK, FULL), BF16),
            pltpu.VMEM((8, ROWS, FULL), BF16),
            pltpu.VMEM((2, ROWS, 128), F32),
            pltpu.VMEM((ROWS, MAIN), F32),
            pltpu.VMEM((ROWS, 2 * REST), F32),
            pltpu.VMEM((ROWS, 6 * CHUNK), F32),
            pltpu.SemaphoreType.DMA((5, ALL, 2)),
            pltpu.SemaphoreType.DMA((5, ALL, 2)),
            pltpu.SemaphoreType.DMA((2,)),
        ],
        compiler_params=pltpu.CompilerParams(
            collective_id=0, has_side_effects=True, vmem_limit_bytes=48 * 2**20
        ),
        name="gather_and_grad",
    )(img_embed, txt_embed)


def solution(mesh):
    return jax.shard_map(
        local,
        mesh=mesh,
        in_specs=(P("batch", "mp"), P("batch", "mp")),
        out_specs=(P("batch", "mp"), P("batch", "mp")),
        check_vma=False,
    )
```

```python
import jax
import jax.numpy as jnp
from jax import lax
from jax.experimental import pallas as pl
from jax.experimental.pallas import tpu as pltpu
from jax.sharding import PartitionSpec as P

MESH = pl.DeviceIdType.MESH
BF16, F32 = jnp.bfloat16, jnp.float32

logit_scale = 100.0
logit_bias = -5.0
norm_eps = 1e-06

ROWS = 512
HALF = 576
MAIN = 512
REST = HALF - MAIN
FULL = 2 * HALF
CHUNK = 32
PACK = CHUNK // 2
STEPS = ROWS // 2 // CHUNK
ALL = 2 * STEPS
AHEAD = 3
LAND, RELAY, CHIP, CALC = 1, 2, 3, 4
LEG1, LEG2, HALO, VIA, PAIR = range(5)


def nt(left, right):
    return lax.dot_general(left, right, (((1,), (1,)), ((), ())), preferred_element_type=F32)


def weigh(scores):
    return 1.0 / (1.0 + jnp.exp(-(logit_scale * scores + logit_bias)))


def kernel(
    img_hbm, txt_hbm, img_out, txt_out, img_ref, txt_ref, stage, land, full, inverse, txt_main, txt_rest, txt_inner,
    sent, came, load,
):
    batch, side = lax.axis_index("batch"), lax.axis_index("mp")
    core = lax.rem(batch, 2)
    y = lax.rem(lax.div(batch, 2), 4)
    z_lo = lax.rem(lax.div(batch, 8), 8)
    x = lax.div(batch, 64)
    z = side * 8 + z_lo

    def device(x, y, z, core):
        x, y, z = lax.rem(x + 4, 4), lax.rem(y + 4, 4), lax.rem(z + 16, 16)
        return (((x * 8 + lax.rem(z, 8)) * 4 + y) * 2 + core, lax.div(z, 8))

    def along_z(distance):
        return device(x, y, z + distance, core)

    x_next = x + lax.div(z_lo, 7)
    x_before = x - 1 + lax.div(z_lo + 7, 8)

    barrier = pltpu.get_barrier_semaphore()

    def greet(where):
        pl.semaphore_signal(barrier, inc=1, device_id=where, device_id_type=MESH)

    for distance in (1, -1, 7, -7):
        greet(along_z(distance))
    greet(device(x, y, z, 1 - core))
    for distance in (1, 2, 3):
        greet(device(x, y + distance, z, core))

    @pl.when(y == 0)
    def _():
        for column in range(4):
            greet(device(x_before, column, z - 1, core))

    @pl.when(y == 3)
    def _():
        for column in range(4):
            greet(device(x_next, column, z + 1, core))

    lane = lax.broadcasted_iota(jnp.int32, (PACK, 2 * REST), 1)

    txt_load = pltpu.make_async_copy(txt_hbm, txt_ref, load.at[0])
    img_load = pltpu.make_async_copy(img_hbm, img_ref, load.at[1])
    txt_load.start()
    img_load.start()

    def pack(ref, array):
        def one(chunk, carry):
            row = pl.multiple_of(chunk * CHUNK, CHUNK)
            low = ref[pl.ds(row, PACK), :]
            high = ref[pl.ds(row + PACK, PACK), :]
            stage[array, chunk, :, :MAIN] = low[:, :MAIN]
            stage[array, chunk, :, MAIN : 2 * MAIN] = high[:, :MAIN]
            stage[array, chunk, :, 2 * MAIN :] = jnp.concatenate([low[:, MAIN:], high[:, MAIN:]], axis=1)
            return carry

        lax.fori_loop(0, 2 * STEPS, one, 0)

    txt_load.wait()
    pack(txt_ref, 0)
    pl.semaphore_wait(barrier, 10)

    def split(t):
        return lax.div(t, STEPS), lax.rem(t, STEPS)

    def copy(kind, t, way, source, target, where):
        return pltpu.make_async_remote_copy(
            src_ref=source,
            dst_ref=target,
            send_sem=sent.at[kind, t, way],
            recv_sem=came.at[kind, t, way],
            device_id=where,
            device_id_type=MESH,
        )

    def first_leg(t, way):
        array, step = split(t)
        chunk = way * STEPS + step
        return copy(LEG1, t, way, stage.at[array, chunk], land.at[0, array, chunk], along_z(7 - 14 * way))

    def second_leg(t, way):
        array, step = split(t)
        chunk = way * STEPS + step
        return copy(LEG2, t, way, land.at[0, array, chunk], land.at[1, array, chunk], along_z(1 - 2 * way))

    def rows_of(t, way):
        array, step = split(t)
        return pl.ds(pl.multiple_of(way * (ROWS // 2) + step * CHUNK, CHUNK), CHUNK)

    def mirror(array, column):
        return column + array * (3 - 2 * column)

    def via_column(t, way):
        array, step = split(t)
        spread = lax.rem(2 * step + way, 4)
        late = lax.div(step, STEPS - 2)
        others = lax.rem(2 * step + way, 3)
        return spread + array * (others + late * (3 - others) - spread)

    def edge(array):
        return device(x_next + array * (x_before - x_next), 3 * array, z + 1 - 2 * array, core)

    def halo(t, way, where, source, target, kind):
        array, step = split(t)
        rows = rows_of(t, way)
        return copy(kind, t, way, full.at[source, rows], full.at[target, rows], where)

    def halo_start(t, way):
        array, step = split(t)
        own, next_one = 3 * array, 3 * array + 2
        place = mirror(array, y)
        via = via_column(t, way)

        @pl.when(place < 3)
        def _():
            halo(t, way, device(x, y + 1 - 2 * array, z, core), own, next_one, HALO).start()

        @pl.when(jnp.logical_and(place == 3, via == 3))
        def _():
            halo(t, way, edge(array), own, next_one, HALO).start()

        @pl.when(jnp.logical_and(place == 3, via < 3))
        def _():
            rows = rows_of(t, way)
            pltpu.make_async_remote_copy(
                src_ref=full.at[own, rows],
                dst_ref=full.at[6 + array, rows],
                send_sem=sent.at[HALO, t, way],
                recv_sem=came.at[VIA, t, way],
                device_id=device(x, mirror(array, via), z, core),
                device_id_type=MESH,
            ).start()

    def on_relay(t, way):
        array, step = split(t)
        via = via_column(t, way)
        return jnp.logical_and(mirror(array, y) == via, via < 3)

    def relay_copy(t, way):
        array, step = split(t)
        rows = rows_of(t, way)
        return pltpu.make_async_remote_copy(
            src_ref=full.at[6 + array, rows],
            dst_ref=full.at[3 * array + 2, rows],
            send_sem=sent.at[VIA, t, way],
            recv_sem=came.at[HALO, t, way],
            device_id=edge(array),
            device_id_type=MESH,
        )

    def pair_copy(t, way):
        array, step = split(t)
        source = 3 * array + 2 * (core + array * (1 - 2 * core))
        return halo(t, way, device(x, y, z, 1 - core), source, 3 * array + 1, PAIR)

    def arrive(t, way):
        array, step = split(t)
        chunk = way * STEPS + step
        row = pl.multiple_of(way * (ROWS // 2) + step * CHUNK, CHUNK)
        mine = stage[array, chunk].astype(F32)
        other = land[1, array, chunk].astype(F32)
        square = mine * mine + other * other
        rest_square = square[:, 2 * MAIN :]
        first = jnp.where(side == 0, mine[:, 2 * MAIN :], other[:, 2 * MAIN :])
        second = jnp.where(side == 0, other[:, 2 * MAIN :], mine[:, 2 * MAIN :])
        for part in range(2):
            total = jnp.sum(square[:, part * MAIN : (part + 1) * MAIN], axis=1, keepdims=True)
            inside = (lane < REST) if part == 0 else (lane >= REST)
            total = total + jnp.sum(jnp.where(inside, rest_square, 0.0), axis=1, keepdims=True)
            scale = lax.rsqrt(total + norm_eps)
            rows = pl.ds(pl.multiple_of(row + part * PACK, PACK), PACK)
            inverse[array, rows, :] = jnp.broadcast_to(scale, (PACK, 128))
            own = 3 * array
            mine_at = pl.ds(pl.multiple_of(side * MAIN, MAIN), MAIN)
            other_at = pl.ds(pl.multiple_of((1 - side) * MAIN, MAIN), MAIN)
            columns = slice(part * MAIN, (part + 1) * MAIN)
            full[own, rows, mine_at] = (mine[:, columns] * scale).astype(BF16)
            full[own, rows, other_at] = (other[:, columns] * scale).astype(BF16)
            if part == 0:
                rest = jnp.where(lane < REST, first, pltpu.roll(second, REST, 1))
            else:
                rest = jnp.where(lane < REST, pltpu.roll(first, REST, 1), second)
            full[own, rows, 2 * MAIN :] = (rest * scale).astype(BF16)

    main_at = pl.ds(pl.multiple_of(side * MAIN, MAIN), MAIN)

    def own_rest(rest):
        return jnp.where(side == 0, rest, pltpu.roll(rest, REST, 1))[:, :REST]

    def finish(ref, out, array, rows, main, rest, inner):
        scale = inverse[array, rows, :][:, :1]
        inner = logit_scale * inner
        values = ref[rows, :].astype(F32)
        unit = values[:, :MAIN] * scale
        out[rows, :MAIN] = ((logit_scale * main - unit * inner) * scale).astype(BF16)
        unit = values[:, MAIN:] * scale
        out[rows, MAIN:] = ((logit_scale * own_rest(rest) - unit * inner) * scale).astype(BF16)

    def images(t):
        both = [rows_of(t, way) for way in range(2)]
        array, step = split(t)
        block = jnp.concatenate([full[3, rows, :] for rows in both], axis=0)
        shape = (2 * CHUNK, ROWS)
        row = lax.broadcasted_iota(jnp.int32, shape, 0)
        row = row + step * CHUNK + jnp.where(row < CHUNK, 0, ROWS // 2 - CHUNK)
        matching = row == lax.broadcasted_iota(jnp.int32, shape, 1)
        main = jnp.zeros((2 * CHUNK, MAIN), F32)
        rest = jnp.zeros((2 * CHUNK, 2 * REST), F32)
        inner = jnp.zeros((2 * CHUNK, 1), F32)
        for offset in range(3):
            scores = nt(block, full[offset])
            weights = weigh(scores)
            if offset == 0:
                weights = jnp.where(matching, weights - 1.0, weights)
            inner = inner + jnp.sum(weights * scores, axis=1, keepdims=True)
            weights = weights.astype(BF16)
            main = main + jnp.dot(weights, full[offset, :, main_at], preferred_element_type=F32)
            rest = rest + jnp.dot(weights, full[offset, :, 2 * MAIN :], preferred_element_type=F32)
        for way, rows in enumerate(both):
            part = slice(way * CHUNK, (way + 1) * CHUNK)
            finish(img_ref, img_out, 1, rows, main[part], rest[part], inner[part])

    def captions(t):
        both = [rows_of(t, way) for way in range(2)]
        array, step = split(t)
        wide = 6 * CHUNK
        block = jnp.concatenate([full[3 + offset, rows, :] for offset in range(3) for rows in both], axis=0)
        block_main = jnp.concatenate([full[3 + offset, rows, main_at] for offset in range(3) for rows in both], axis=0)
        shape = (ROWS, wide)
        column = lax.broadcasted_iota(jnp.int32, shape, 1)
        place = column + step * CHUNK + jnp.where(column < CHUNK, 0, ROWS // 2 - CHUNK)
        matching = jnp.logical_and(column < 2 * CHUNK, place == lax.broadcasted_iota(jnp.int32, shape, 0))
        scores = nt(full[0], block)
        weights = weigh(scores)
        weights = jnp.where(matching, weights - 1.0, weights)
        txt_inner[...] += weights * scores
        weights = weights.astype(BF16)
        txt_main[...] += jnp.dot(weights, block_main, preferred_element_type=F32)
        txt_rest[...] += jnp.dot(weights, block[:, 2 * MAIN :], preferred_element_type=F32)

    for t in range(AHEAD):
        for way in range(2):
            first_leg(t, way).start()

    img_load.wait()
    pack(img_ref, 1)
    txt_main[...] = jnp.zeros_like(txt_main)
    txt_rest[...] = jnp.zeros_like(txt_rest)
    txt_inner[...] = jnp.zeros_like(txt_inner)

    def during(t, body):
        @pl.when(jnp.logical_and(t >= 0, t < ALL))
        def _():
            for way in range(2):
                body(t, way)

    def done_before(now):
        level = lax.div(now, ALL - 1)
        return (2 * now - ALL + 1) * (1 - level) + (now - 1) * level

    def step(now, carry):
        def pass_on(t, way):
            first_leg(t, way).wait_recv()
            second_leg(t, way).start()

        during(now, pass_on)

        def take(t, way):
            second_leg(t, way).wait_recv()
            arrive(t, way)
            halo_start(t, way)

        during(now - LAND, take)

        def relay(t, way):
            @pl.when(on_relay(t, way))
            def _():
                array, _ = split(t)
                rows = rows_of(t, way)
                halo(t, way, along_z(1), 6 + array, 6 + array, VIA).wait_recv()
                relay_copy(t, way).start()

        during(now - RELAY, relay)
        during(now + AHEAD, lambda t, way: first_leg(t, way).start())

        def to_pair(t, way):
            array, _ = split(t)
            halo(t, way, along_z(1), 3 * array, 3 * array + 2, HALO).wait_recv()
            pair_copy(t, way).start()

        during(now - CHIP, to_pair)
        during(now - CALC, lambda t, way: pair_copy(t, way).wait_recv())
        before = now - CALC

        @pl.when(jnp.logical_and(before >= STEPS, before < ALL))
        def _():
            captions(before)

        @pl.when(jnp.logical_and(now >= STEPS + CHIP, now <= ALL))
        def _():
            def rows(t, carry):
                @pl.when(t >= STEPS)
                def _():
                    images(t)

                return carry

            lax.fori_loop(done_before(now), done_before(now + 1), rows, 0)

        return carry

    lax.fori_loop(0, ALL + CALC, step, 0)

    def last(block, carry):
        rows = pl.ds(pl.multiple_of(block * 64, 64), 64)
        inner = jnp.sum(txt_inner[rows, :], axis=1, keepdims=True)
        finish(txt_ref, txt_out, 0, rows, txt_main[rows, :], txt_rest[rows, :], inner)
        return carry

    lax.fori_loop(0, ROWS // 64, last, 0)

    def drain(t, carry):
        array, _ = split(t)
        for way in range(2):
            first_leg(t, way).wait_send()
            second_leg(t, way).wait_send()
            halo(t, way, along_z(1), 3 * array, 3 * array + 2, HALO).wait_send()
            pair_copy(t, way).wait_send()

            @pl.when(on_relay(t, way))
            def _():
                relay_copy(t, way).wait_send()

        return carry

    lax.fori_loop(0, ALL, drain, 0)


def local(img_embed, txt_embed):
    vmem = pl.BlockSpec(memory_space=pltpu.VMEM)
    return pl.pallas_call(
        kernel,
        out_shape=(jax.ShapeDtypeStruct((ROWS, HALF), BF16),) * 2,
        in_specs=[pl.BlockSpec(memory_space=pl.ANY)] * 2,
        out_specs=(vmem, vmem),
        scratch_shapes=[
            pltpu.VMEM((ROWS, HALF), BF16),
            pltpu.VMEM((ROWS, HALF), BF16),
            pltpu.VMEM((2, 2 * STEPS, PACK, FULL), BF16),
            pltpu.VMEM((2, 2, 2 * STEPS, PACK, FULL), BF16),
            pltpu.VMEM((8, ROWS, FULL), BF16),
            pltpu.VMEM((2, ROWS, 128), F32),
            pltpu.VMEM((ROWS, MAIN), F32),
            pltpu.VMEM((ROWS, 2 * REST), F32),
            pltpu.VMEM((ROWS, 6 * CHUNK), F32),
            pltpu.SemaphoreType.DMA((5, ALL, 2)),
            pltpu.SemaphoreType.DMA((5, ALL, 2)),
            pltpu.SemaphoreType.DMA((2,)),
        ],
        compiler_params=pltpu.CompilerParams(
            collective_id=0, has_side_effects=True, vmem_limit_bytes=48 * 2**20
        ),
        name="gather_and_grad",
    )(img_embed, txt_embed)


def solution(mesh):
    return jax.shard_map(
        local,
        mesh=mesh,
        in_specs=(P("batch", "mp"), P("batch", "mp")),
        out_specs=(P("batch", "mp"), P("batch", "mp")),
        check_vma=False,
    )
```
